128 devices in a mesh: stn: 16 (over y, x), chan: 4 (over z), beam: 2 (over core).
Axes of the slice: x: 4, y: 4, z: 4, core: 2. Of those that a mesh axis runs over, the one named last changes fastest.
Arguments:
- volts: bfloat16 [2, 512, 12, 9216], P(None, 'stn', 'chan', 'beam'), may hold values from -6 to 6
- taps: float32 [16, 256], replicated, may hold values from -1.5 to 1.5
- delays: int32 [128, 512], P(None, 'stn'), may hold values from 0 to 1023
- station_sub: int32 [512], P('stn'), may hold values from 0 to 3
- beam_sub: int32 [128], replicated, may hold values from 0 to 3
Outputs:
- beams: float32 [128, 2, 12, 48, 256], P(('stn', 'chan', 'beam'))
The draws below stay inside these ranges and needn't reach their ends.
All inputs are finite; a program needn't handle non-finite values.
Results may differ from the reference program's by a relative error of at most 0.014.
Values may be sent and summed in bfloat16 or wider, within the bound.
No kernel may reach another device: no remote copies, remote signals or barrier semaphores. Data moves between devices by JAX's collectives and lax.ppermute only.
A program may use at most 192 MiB of HBM per device.

```python
import math
import jax
import jax.numpy as jnp
from jax import lax

FINE = 256
TAPS = 16
STN_DEV = 32
SUBARRAYS = 4
STATIONS = 512
CHANNELS = 12
FRAMES = 48
SAMPLES = 9216
BEAMS = 128
N_STN = 16


def set_ends(drawn, key, low, top_value):
    dims = drawn.shape
    spot = [jax.random.randint(jax.random.fold_in(key, axis), (), 0, dims[axis]) for axis in range(len(dims))]
    drawn = drawn.at[tuple(spot)].set(low)
    longest = dims.index(max(dims))
    spot[longest] = (spot[longest] + 1) % dims[longest]
    return drawn.at[tuple(spot)].set(top_value)


def steps_of(own_key, extent, shards, low, high):
    loudness, own = 1.0, jax.random.fold_in(own_key, 6)
    for position, blocks in shards:
        steps = jnp.exp(jax.random.uniform(jax.random.fold_in(own, position), (blocks,), jnp.float32, low / len(shards), high / len(shards)))
        loudness = loudness * jnp.repeat(steps, extent[position] // blocks).reshape([-1 if axis == position else 1 for axis in range(len(extent))])
    return loudness


def noise(rng, shape, scale, limit, cuts=(), kind=jnp.bfloat16):
    factor_of = steps_of(rng, shape, cuts, -0.22, 0.18) if cuts else 1.0
    values = jax.random.normal(rng, shape, jnp.float32) * scale * factor_of
    return jnp.minimum(jnp.maximum(values, -limit), limit).astype(kind)


def setup_inputs(seed: int = 0) -> dict:
    arg_keys = jax.random.split(jax.random.key(seed), 6)
    return {
        "volts": noise(arg_keys[0], (2, STATIONS, CHANNELS, SAMPLES), 1.0, 6.0, ((1, 16), (2, 4), (3, 2))),
        "taps": noise(arg_keys[1], (TAPS, FINE), 0.25, 1.5, (), jnp.float32),
        "delays": set_ends(jax.random.randint(arg_keys[2], (BEAMS, STATIONS), 0, 1024), jax.random.fold_in(arg_keys[2], 1), 0, 1023).astype(jnp.int32),
        "station_sub": set_ends(jax.random.randint(arg_keys[3], (STATIONS,), 0, SUBARRAYS), jax.random.fold_in(arg_keys[3], 1), 0, SUBARRAYS - 1).astype(jnp.int32),
        "beam_sub": set_ends(jax.random.randint(arg_keys[4], (BEAMS,), 0, SUBARRAYS), jax.random.fold_in(arg_keys[4], 1), 0, SUBARRAYS - 1).astype(jnp.int32),
    }


def filter_frames(extended, taps, frame_count):
    tap_count, fine = taps.shape
    hop = 3 * fine // 4
    groups = frame_count // 4
    rows = groups + (tap_count + 2) // 3
    shape = extended.shape
    needed = 3 * hop + 3 * rows * fine
    padding = max(0, needed - shape[-1])
    padded = jnp.concatenate([extended, jnp.zeros(shape[:-1] + (padding,), extended.dtype)], axis=-1)
    streams = []
    for phase in range(4):
        start = phase * hop
        piece = lax.slice_in_dim(padded, start, start + 3 * rows * fine, 1, len(shape) - 1)
        streams.append(piece.reshape(shape[:-1] + (rows, 3, fine)))
    stacked = jnp.stack(streams, axis=-2)
    axis = len(shape) - 1
    total = None
    for tap in range(tap_count):
        lead = tap // 3
        inner = tap % 3
        window = lax.slice_in_dim(stacked, lead, lead + groups, 1, axis)[..., inner, :, :].astype(jnp.float32)
        term = taps[tap] * window
        total = term if total is None else total + term
    return total.reshape(shape[:-1] + (frame_count, fine)).astype(jnp.bfloat16)

def dft_tables(fine):
    index = jnp.arange(fine, dtype=jnp.int32)
    product = index[:, None] * index[None, :] % fine
    angle = 2.0 * jnp.pi * product.astype(jnp.float32) / fine
    scale = 1.0 / math.sqrt(fine)
    return ((jnp.cos(angle) * scale).astype(jnp.bfloat16), (jnp.sin(angle) * scale).astype(jnp.bfloat16))

def channelize(filtered, frame_start, hop):
    fine = filtered.shape[-1]
    cosine, sine = dft_tables(fine)
    spec_re = jnp.einsum('...j,jk->...k', filtered[0], cosine, preferred_element_type=jnp.float32) + jnp.einsum('...j,jk->...k', filtered[1], sine, preferred_element_type=jnp.float32)
    spec_im = jnp.einsum('...j,jk->...k', filtered[1], cosine, preferred_element_type=jnp.float32) - jnp.einsum('...j,jk->...k', filtered[0], sine, preferred_element_type=jnp.float32)
    frame_count = filtered.shape[-2]
    frame_index = frame_start + jnp.arange(frame_count, dtype=jnp.int32)
    fine_index = jnp.arange(fine, dtype=jnp.int32)
    turn = fine_index[None, :] * hop % fine * frame_index[:, None] % fine
    rot = 2.0 * jnp.pi * turn.astype(jnp.float32) / fine
    cos_rot = jnp.cos(rot)
    sin_rot = jnp.sin(rot)
    out_re = spec_re * cos_rot + spec_im * sin_rot
    out_im = spec_im * cos_rot - spec_re * sin_rot
    return jnp.stack([out_re, out_im]).astype(jnp.bfloat16)

def steering(delay_rows, beam_subs, station_subs, chan_start, chan_count, fine, amplitude):
    fine_index = jnp.arange(fine, dtype=jnp.int32)
    chan_index = chan_start + jnp.arange(chan_count, dtype=jnp.int32)
    freq_index = chan_index[:, None] * fine + fine_index[None, :]
    turn = delay_rows[:, :, None, None] * freq_index[None, None, :, :] % 65536
    phase = 2.0 * jnp.pi * turn.astype(jnp.float32) / 65536.0
    member = (beam_subs[:, None] == station_subs[None, :]).astype(jnp.float32)[:, :, None, None]
    weight_re = (amplitude * member * jnp.cos(phase)).astype(jnp.bfloat16)
    weight_im = (-amplitude * member * jnp.sin(phase)).astype(jnp.bfloat16)
    return (weight_re, weight_im)

def reference(volts, taps, delays, station_sub, beam_sub):
    hop = 3 * FINE // 4
    extra = TAPS * FINE - hop
    amplitude = 1.0 / math.sqrt(STATIONS // SUBARRAYS)

    def one_channel(chan):
        raw = lax.dynamic_slice_in_dim(volts, chan, 1, 2)
        extended = jnp.concatenate([raw, jnp.zeros((2, STATIONS, 1, extra), jnp.bfloat16)], axis=3)
        filtered = filter_frames(extended, taps, FRAMES)
        spectra = channelize(filtered, 0, hop)
        weight_re, weight_im = steering(delays, beam_sub, station_sub, chan, 1, FINE, amplitude)
        grouped = spectra.reshape(2, N_STN, STN_DEV, 1, FRAMES, FINE).astype(jnp.float32)
        w_re = weight_re.reshape(BEAMS, N_STN, STN_DEV, 1, FINE).astype(jnp.float32)
        w_im = weight_im.reshape(BEAMS, N_STN, STN_DEV, 1, FINE).astype(jnp.float32)
        form = 'bgsck,gscfk->gbcfk'
        part_re = jnp.einsum(form, w_re, grouped[0]) - jnp.einsum(form, w_im, grouped[1])
        part_im = jnp.einsum(form, w_re, grouped[1]) + jnp.einsum(form, w_im, grouped[0])
        part_re = part_re.astype(jnp.bfloat16).astype(jnp.float32)
        part_im = part_im.astype(jnp.bfloat16).astype(jnp.float32)
        total_re = lax.optimization_barrier(jnp.sum(part_re, axis=0))[:, 0]
        total_im = lax.optimization_barrier(jnp.sum(part_im, axis=0))[:, 0]
        return jnp.stack([total_re, total_im], axis=1)
    per_channel = lax.map(one_channel, jnp.arange(CHANNELS, dtype=jnp.int32))
    return jnp.transpose(per_channel, (1, 2, 0, 3, 4))
```

```python
import functools
import math

import jax
import jax.numpy as jnp
from jax import lax
from jax.experimental import pallas as pl
from jax.experimental.pallas import tpu as pltpu
from jax.sharding import PartitionSpec as P

SUBARRAYS = 4
F32 = jnp.float32
BF16 = jnp.bfloat16
LANES = 128
NT = (((1,), (1,)), ((), ()))
NN = (((1,), (0,)), ((), ()))
START = (0, 0, 1, 2)
OFFSET = (0, 192, 128, 64)


def filter_tables(taps):
    count, fine = taps.shape
    lane = jnp.arange(fine, dtype=jnp.int32)
    tables = []
    for offset in OFFSET:
        rolled = jnp.roll(taps, offset, axis=1)
        early = jnp.pad(rolled, ((0, 1), (0, 0)))
        late = jnp.pad(rolled, ((1, 0), (0, 0)))
        tables.append(jnp.where(lane[None, :] >= offset, early, late))
    joined = jnp.concatenate(tables)
    return jnp.broadcast_to(joined[:, None, :], (joined.shape[0], 8, fine))


def dft_table(fine):
    index = jnp.arange(fine, dtype=jnp.int32)
    product = index[:, None] * index[None, :] % fine
    angle = 2.0 * jnp.pi * product.astype(F32) / fine
    scale = 1.0 / math.sqrt(fine)
    return jnp.concatenate(
        [(jnp.cos(angle) * scale).astype(BF16), (jnp.sin(angle) * scale).astype(BF16)], axis=1
    )


def tap_range(phase, tile, count):
    low, high = tile * LANES, (tile + 1) * LANES
    first = 1 if high <= OFFSET[phase] else 0
    last = count - 1 if low >= OFFSET[phase] else count
    return first, last


def channelize_kernel(count, core_ref, own_ref, other_ref, taps_ref, dft_ref, out_ref, x_ref, z_ref):
    half = own_ref.shape[-1]
    fine = taps_ref.shape[-1]
    blocks = 2 * half // fine
    groups = blocks // 3
    core = core_ref[0]
    own_at = pl.multiple_of(core * half, LANES)
    other_at = pl.multiple_of((1 - core) * half, LANES)
    own_row = pl.multiple_of(core * 16, 16)
    for part in range(2):
        x_ref[part, :, pl.ds(own_at, half)] = own_ref[part, 0, pl.ds(own_row, 16), :]
        x_ref[part, :, pl.ds(other_at, half)] = other_ref[part, 0]
    frames = 4 * groups
    rows = 2 * frames
    tiles = fine // LANES
    for tile in range(tiles):
        for group in range(groups):
            sums = [[[None, None] for _ in range(2)] for _ in range(4)]
            for step in range(count + 3):
                block = 3 * group + step
                if block >= blocks:
                    break
                uses = []
                for phase in range(4):
                    first, last = tap_range(phase, tile, count)
                    tap = step - START[phase]
                    if first <= tap <= last:
                        uses.append((phase, tap))
                if not uses:
                    continue
                at = block * fine + tile * LANES
                data = [x_ref[part, :, pl.ds(at, LANES)].astype(F32) for part in range(2)]
                for phase, tap in uses:
                    weight = taps_ref[phase * (count + 1) + tap, :, pl.ds(tile * LANES, LANES)]
                    for part in range(2):
                        for side in range(2):
                            term = weight * data[part][8 * side : 8 * side + 8]
                            old = sums[phase][part][side]
                            sums[phase][part][side] = term if old is None else old + term
            for phase in range(4):
                frame = 4 * group + phase
                for side in range(2):
                    real, imag = sums[phase][0][side], sums[phase][1][side]
                    base = side * 8 * rows + frame
                    top = pl.ds(base, 8, stride=rows)
                    low = pl.ds(base + frames, 8, stride=rows)
                    z_ref[tile, top, :] = real
                    z_ref[tiles + tile, top, :] = imag
                    z_ref[tile, low, :] = imag
                    z_ref[tiles + tile, low, :] = -real
    table = dft_ref[...]
    piece = rows // 3
    dests = out_ref.shape[0]
    for pair in range(2):
        results = []
        for quad in (2 * pair, 2 * pair + 1):
            order = []
            for member in range(3):
                start = (4 * quad + member) * rows
                order.append((start, rows))
                order.append(((4 * quad + 3) * rows + member * piece, piece))
            operand = jnp.concatenate(
                [
                    jnp.concatenate(
                        [z_ref[lane, pl.ds(start, size), :] for lane in range(2 * tiles)], axis=1
                    ).astype(BF16)
                    for start, size in order
                ],
                axis=0,
            )
            found = lax.dot_general(table, operand, NT, preferred_element_type=F32)
            results.append(found.reshape(dests, fine // dests, 4 * rows))
        out_ref[:, 0, pl.ds(16 * pair, 16), :] = jnp.concatenate(results, axis=1).astype(BF16)


def turn_parts(turn):
    quadrant = lax.shift_right_logical(turn + 8192, 14)
    x = (turn - quadrant * 16384).astype(F32) * (2.0 * math.pi / 65536.0)
    y = x * x
    sine = x * (1.0 + y * (-1.0 / 6 + y * (1.0 / 120 + y * (-1.0 / 5040 + y * (1.0 / 362880)))))
    cosine = 1.0 + y * (-0.5 + y * (1.0 / 24 + y * (-1.0 / 720 + y * (1.0 / 40320))))
    odd = (quadrant & 1) == 1
    cos_part = jnp.where(odd, sine, cosine)
    sin_part = jnp.where(odd, cosine, sine)
    cos_part = jnp.where(((quadrant + 1) & 2) == 2, -cos_part, cos_part)
    sin_part = jnp.where((quadrant & 2) == 2, -sin_part, sin_part)
    return cos_part, sin_part


def beam_kernel(
    amplitude, fine, place_ref, code_ref, data_ref, out_ref, delay_ref, flat_ref, weight_ref, sum_ref
):
    coarse = pl.program_id(0)
    sources = data_ref.shape[0]
    beams = out_ref.shape[0]
    near = out_ref.shape[2]
    quads = data_ref.shape[2] // near
    depth = sources * quads
    stations = 4 * depth

    @pl.when(coarse == 0)
    def _():
        for member in range(4):
            for index in range(code_ref.shape[0]):
                width = code_ref.shape[2]
                delay_ref[pl.ds(member * depth + index * width, width), :] = code_ref[index, member]

    freq = (place_ref[0] + coarse) * fine + place_ref[1]
    strip = 32
    for member in range(4):
        lanes = pl.ds(member * depth, depth)
        turned = jnp.transpose(delay_ref[lanes, :].astype(F32)).astype(jnp.int32)
        for top in range(0, beams, strip):
            delay = turned[top : top + strip]
            scale = jnp.where(delay >= 0, amplitude, 0.0).astype(F32)
            delay = jnp.maximum(delay, 0)
            cos_part, sin_part = turn_parts((delay * freq) & 65535)
            cos_step, sin_step = turn_parts(delay)
            real, imag = cos_part * scale, -(sin_part * scale)
            for step in range(near):
                weight_ref[step, pl.ds(top, strip), lanes] = real.astype(BF16)
                weight_ref[step, pl.ds(beams + top, strip), lanes] = imag.astype(BF16)
                if step + 1 < near:
                    real, imag = (
                        real * cos_step + imag * sin_step,
                        imag * cos_step - real * sin_step,
                    )

    for tile in range(3):
        flat_ref[tile] = (
            data_ref[:, 0, :, pl.ds(tile * LANES, LANES)]
            .astype(F32)
            .reshape(sources * quads * near, LANES)
        )
    lane = lax.broadcasted_iota(jnp.int32, (depth, LANES), 1)
    lane_out = lax.broadcasted_iota(jnp.int32, (beams, LANES), 1)
    for step in range(near):
        pieces = [flat_ref[tile, pl.ds(step, depth, stride=near), :] for tile in range(3)]
        last = jnp.where(
            lane < 32,
            pltpu.roll(pieces[0], 32, 1),
            jnp.where(lane < 64, pltpu.roll(pieces[1], 64, 1), pltpu.roll(pieces[2], 96, 1)),
        )
        operand = jnp.concatenate([piece.astype(BF16) for piece in pieces + [last]], axis=0)
        found = lax.dot_general(weight_ref[step], operand, NN, preferred_element_type=F32)
        by_real, by_imag = found[:beams], found[beams:]
        crossed = jnp.where(lane_out < 48, -pltpu.roll(by_imag, 80, 1), pltpu.roll(by_imag, 48, 1))
        sum_ref[pl.ds(step, beams, stride=near), :] = by_real + crossed
    out_ref[:, 0] = sum_ref[...].reshape(beams, near, LANES).astype(BF16)


def order_kernel(data_ref, out_ref):
    coarse, frames, fine = out_ref.shape[2:]
    width = 2 * frames
    row = lax.broadcasted_iota(jnp.int32, (width, LANES), 0)
    column = lax.broadcasted_iota(jnp.int32, (width, LANES), 1)
    unit = (row == column).astype(F32).astype(BF16)
    keep = lax.broadcasted_iota(jnp.int32, (fine, LANES), 1) < width
    for index in range(coarse):
        block = data_ref[:, 0, :, index].astype(F32).reshape(fine, LANES)
        block = jnp.where(keep, block, 0.0).astype(BF16)
        found = lax.dot_general(unit, block, NT, preferred_element_type=F32)
        out_ref[0, 0, index] = found[:frames]
        out_ref[0, 1, index] = found[frames:]


def body(volts, taps, delays, station_sub, beam_sub):
    count, fine = taps.shape
    stations, coarse, half = volts.shape[1:]
    beams = beam_sub.shape[0]
    stn, chan, beam = (lax.axis_size(name) for name in ("stn", "chan", "beam"))
    core = lax.axis_index("beam")
    dests = stn * beam
    near = fine // dests
    frames = beam * half // (3 * fine // 4)
    own = stations // beam
    amplitude = 1.0 / math.sqrt(stations * stn // SUBARRAYS)

    arranged = jnp.transpose(volts, (0, 2, 1, 3))
    away = lax.dynamic_slice_in_dim(arranged, (1 - core) * own, own, 2)
    other = lax.ppermute(away, "beam", [(0, 1), (1, 0)])

    code = jnp.where(station_sub[:, None] == beam_sub[None, :], delays.T, -1)
    code = code.reshape(stations // 4, 4, beams).transpose(1, 0, 2)
    codes = lax.all_gather(code, "stn")

    spectra = pl.pallas_call(
        functools.partial(channelize_kernel, count),
        grid=(coarse,),
        out_shape=jax.ShapeDtypeStruct((dests, coarse, own // 4 * near, 8 * frames), BF16),
        in_specs=[
            pl.BlockSpec(memory_space=pltpu.SMEM),
            pl.BlockSpec((2, 1, stations, half), lambda c: (0, c, 0, 0)),
            pl.BlockSpec((2, 1, own, half), lambda c: (0, c, 0, 0)),
            pl.BlockSpec((4 * (count + 1), 8, fine), lambda c: (0, 0, 0)),
            pl.BlockSpec((fine, 2 * fine), lambda c: (0, 0)),
        ],
        out_specs=pl.BlockSpec((dests, 1, own // 4 * near, 8 * frames), lambda c: (0, c, 0, 0)),
        scratch_shapes=[
            pltpu.VMEM((2, own, beam * half), BF16),
            pltpu.VMEM((2 * fine // LANES, own * 2 * frames, LANES), F32),
        ],
        compiler_params=pltpu.CompilerParams(vmem_limit_bytes=40 * 2**20),
        name="channelize",
    )(core.reshape(1), arranged, other, filter_tables(taps), dft_table(fine))

    mixed = lax.all_to_all(spectra, ("stn", "beam"), 0, 0, tiled=True)

    place = jnp.stack(
        [lax.axis_index("chan") * coarse, (lax.axis_index("stn") * beam + core) * near]
    ).astype(jnp.int32)
    total = stations * stn
    formed = pl.pallas_call(
        functools.partial(beam_kernel, amplitude, fine),
        grid=(coarse,),
        out_shape=jax.ShapeDtypeStruct((beams, coarse, near, LANES), BF16),
        in_specs=[
            pl.BlockSpec(memory_space=pltpu.SMEM),
            pl.BlockSpec((stn, 4, stations // 4, beams), lambda c: (0, 0, 0, 0)),
            pl.BlockSpec((dests, 1, own // 4 * near, 8 * frames), lambda c: (0, c, 0, 0)),
        ],
        out_specs=pl.BlockSpec((beams, 1, near, LANES), lambda c: (0, c, 0, 0)),
        scratch_shapes=[
            pltpu.VMEM((total, beams), jnp.int32),
            pltpu.VMEM((3, total // 4 * near, LANES), F32),
            pltpu.VMEM((near, 2 * beams, total), BF16),
            pltpu.VMEM((beams * near, LANES), F32),
        ],
        compiler_params=pltpu.CompilerParams(vmem_limit_bytes=40 * 2**20),
        name="beamform",
    )(place, codes, mixed)

    owned = lax.all_to_all(formed, ("stn", "chan", "beam"), 0, 0, tiled=True)
    owned = owned.reshape(stn, chan, beam, coarse, near, LANES)
    return pl.pallas_call(
        order_kernel,
        grid=(chan,),
        out_shape=jax.ShapeDtypeStruct((1, 2, chan * coarse, frames, fine), F32),
        in_specs=[
            pl.BlockSpec((stn, 1, beam, coarse, near, LANES), lambda z: (0, z, 0, 0, 0, 0))
        ],
        out_specs=pl.BlockSpec((1, 2, coarse, frames, fine), lambda z: (0, 0, z, 0, 0)),
        compiler_params=pltpu.CompilerParams(vmem_limit_bytes=32 * 2**20),
        name="order",
    )(owned)


def solution(mesh):
    placed = (P(None, "stn", "chan", "beam"), P(), P(None, "stn"), P("stn"), P())
    return jax.shard_map(
        body,
        mesh=mesh,
        in_specs=placed,
        out_specs=P(("stn", "chan", "beam"), None, None, None, None),
        check_vma=False,
    )
```

```python
import functools
import math

import jax
import jax.numpy as jnp
import ml_dtypes
import numpy as np
from jax import lax
from jax.experimental import pallas as pl
from jax.experimental.pallas import tpu as pltpu
from jax.sharding import PartitionSpec as P

SUBARRAYS = 4
F32 = jnp.float32
BF16 = jnp.bfloat16
LANES = 128
PITCH = 9
NT = (((1,), (1,)), ((), ()))
NN = (((1,), (0,)), ((), ()))
START = (0, 0, 1, 2)
OFFSET = (0, 192, 128, 64)


def fill_filter_tables(taps_ref, wide_ref):
    count, fine = taps_ref.shape
    taps = taps_ref[...]
    lane = lax.broadcasted_iota(jnp.int32, (1, fine), 1)
    for phase, offset in enumerate(OFFSET):
        rolled = pltpu.roll(taps, offset, 1) if offset else taps
        for tap in range(count + 1):
            early, late = rolled[min(tap, count - 1)], rolled[max(tap - 1, 0)]
            early = early[None] if tap < count else jnp.zeros((1, fine), F32)
            late = late[None] if tap > 0 else jnp.zeros((1, fine), F32)
            row = jnp.where(lane >= offset, early, late)
            wide_ref[phase * (count + 1) + tap] = jnp.broadcast_to(row, (8, fine))


def dft_table(fine):
    index = np.arange(fine)
    angle = 2.0 * np.pi * (index[:, None] * index[None, :] % fine) / fine
    table = np.concatenate([np.cos(angle), np.sin(angle)], axis=1) / math.sqrt(fine)
    return jnp.asarray(table.astype(np.float32).astype(ml_dtypes.bfloat16))


def tap_range(phase, tile, count):
    low, high = tile * LANES, (tile + 1) * LANES
    first = 1 if high <= OFFSET[phase] else 0
    last = count - 1 if low >= OFFSET[phase] else count
    return first, last


def channelize_kernel(
    core_ref, own_ref, other_ref, prototype_ref, dft_ref, out_ref, x_ref, z_ref, taps_ref
):
    count = prototype_ref.shape[0]

    @pl.when(pl.program_id(0) == 0)
    def _():
        fill_filter_tables(prototype_ref, taps_ref)

    half = own_ref.shape[-1]
    fine = taps_ref.shape[-1]
    blocks = 2 * half // fine
    groups = blocks // 3
    core = core_ref[0]
    own_at = pl.multiple_of(core * half, LANES)
    other_at = pl.multiple_of((1 - core) * half, LANES)
    own_row = pl.multiple_of(core * 16, 16)
    for part in range(2):
        x_ref[part, :, pl.ds(own_at, half)] = own_ref[part, 0, pl.ds(own_row, 16), :]
        x_ref[part, :, pl.ds(other_at, half)] = other_ref[part, 0]
    frames = 4 * groups
    rows = 2 * frames
    depth = PITCH * rows
    tiles = fine // LANES
    for tile in range(tiles):
        for group in range(groups):
            sums = [[[None, None] for _ in range(2)] for _ in range(4)]
            for step in range(count + 3):
                block = 3 * group + step
                if block >= blocks:
                    break
                uses = []
                for phase in range(4):
                    first, last = tap_range(phase, tile, count)
                    tap = step - START[phase]
                    if first <= tap <= last:
                        uses.append((phase, tap))
                if not uses:
                    continue
                at = block * fine + tile * LANES
                data = [x_ref[part, :, pl.ds(at, LANES)].astype(F32) for part in range(2)]
                for phase, tap in uses:
                    weight = taps_ref[phase * (count + 1) + tap, :, pl.ds(tile * LANES, LANES)]
                    for part in range(2):
                        for side in range(2):
                            term = weight * data[part][8 * side : 8 * side + 8]
                            old = sums[phase][part][side]
                            sums[phase][part][side] = term if old is None else old + term
            for phase in range(4):
                frame = 4 * group + phase
                for side in range(2):
                    real, imag = sums[phase][0][side], sums[phase][1][side]
                    base = side * depth + PITCH * frame
                    top = pl.ds(base, 8)
                    low = pl.ds(base + PITCH * frames, 8)
                    z_ref[tile, top, :] = real
                    z_ref[tiles + tile, top, :] = imag
                    z_ref[tile, low, :] = imag
                    z_ref[tiles + tile, low, :] = -real
    table = dft_ref[...]
    piece = rows // 3
    dests = out_ref.shape[0]
    for pair in range(2):
        results = []
        for quad in (2 * pair, 2 * pair + 1):
            order = []
            base = pair * depth + 4 * (quad % 2)
            for member in range(3):
                order.append((base + member, rows))
                order.append((base + 3 + PITCH * member * piece, piece))
            operand = jnp.concatenate(
                [
                    jnp.concatenate(
                        [z_ref[lane, pl.ds(start, size, stride=PITCH), :] for lane in range(2 * tiles)], axis=1
                    ).astype(BF16)
                    for start, size in order
                ],
                axis=0,
            )
            found = lax.dot_general(table, operand, NT, preferred_element_type=F32)
            results.append(found.reshape(dests, fine // dests, 4 * rows))
        out_ref[:, 0, pl.ds(16 * pair, 16), :] = jnp.concatenate(results, axis=1).astype(BF16)


def turn_parts(turn):
    quadrant = lax.shift_right_logical(turn + 8192, 14)
    x = (turn - quadrant * 16384).astype(F32) * (2.0 * math.pi / 65536.0)
    y = x * x
    sine = x * (1.0 + y * (-1.0 / 6 + y * (1.0 / 120 + y * (-1.0 / 5040 + y * (1.0 / 362880)))))
    cosine = 1.0 + y * (-0.5 + y * (1.0 / 24 + y * (-1.0 / 720 + y * (1.0 / 40320))))
    odd = (quadrant & 1) == 1
    cos_part = jnp.where(odd, sine, cosine)
    sin_part = jnp.where(odd, cosine, sine)
    cos_part = jnp.where(((quadrant + 1) & 2) == 2, -cos_part, cos_part)
    sin_part = jnp.where((quadrant & 2) == 2, -sin_part, sin_part)
    return cos_part, sin_part


def weight_kernel(amplitude, fine, place_ref, code_ref, weight_ref, delay_ref):
    near, rows, stations = weight_ref.shape[1:]
    beams = rows // 2
    depth = stations // 4
    coarse = pl.program_id(0)

    @pl.when(coarse == 0)
    def _():
        width = code_ref.shape[2]
        for index in range(code_ref.shape[0]):
            for member in range(4):
                delay_ref[pl.ds(member * depth + index * width, width), :] = code_ref[index, member]

    freq = (place_ref[0] + coarse) * fine + place_ref[1]
    strip = 32
    for member in range(4):
        lanes = pl.ds(member * depth, depth)
        turned = jnp.transpose(delay_ref[lanes, :].astype(F32)).astype(jnp.int32)
        for top in range(0, beams, strip):
            delay = turned[top : top + strip]
            scale = jnp.where(delay >= 0, amplitude, 0.0).astype(F32)
            delay = jnp.maximum(delay, 0)
            cos_part, sin_part = turn_parts((delay * freq) & 65535)
            cos_step, sin_step = turn_parts(delay)
            real, imag = cos_part * scale, -(sin_part * scale)
            for step in range(near):
                weight_ref[0, step, pl.ds(top, strip), lanes] = real.astype(BF16)
                weight_ref[0, step, pl.ds(beams + top, strip), lanes] = imag.astype(BF16)
                if step + 1 < near:
                    real, imag = (
                        real * cos_step + imag * sin_step,
                        imag * cos_step - real * sin_step,
                    )


def beam_kernel(weight_ref, data_ref, out_ref, flat_ref, sum_ref):
    sources = data_ref.shape[0]
    beams = out_ref.shape[0]
    near = out_ref.shape[2]
    quads = data_ref.shape[2] // near
    depth = sources * quads
    for tile in range(3):
        for source in range(sources):
            block = data_ref[source, 0, :, pl.ds(tile * LANES, LANES)].astype(F32)
            for quad in range(quads):
                row = PITCH * (source * quads + quad)
                flat_ref[tile, pl.ds(row, near), :] = block[quad * near : (quad + 1) * near]
    lane = lax.broadcasted_iota(jnp.int32, (depth, LANES), 1)
    lane_out = lax.broadcasted_iota(jnp.int32, (beams, LANES), 1)
    for step in range(near):
        pieces = [flat_ref[tile, pl.ds(step, depth, stride=PITCH), :] for tile in range(3)]
        last = jnp.where(
            lane < 32,
            pltpu.roll(pieces[0], 32, 1),
            jnp.where(lane < 64, pltpu.roll(pieces[1], 64, 1), pltpu.roll(pieces[2], 96, 1)),
        )
        operand = jnp.concatenate([piece.astype(BF16) for piece in pieces + [last]], axis=0)
        found = lax.dot_general(weight_ref[0, step], operand, NN, preferred_element_type=F32)
        by_real, by_imag = found[:beams], found[beams:]
        crossed = jnp.where(lane_out < 48, -pltpu.roll(by_imag, 80, 1), pltpu.roll(by_imag, 48, 1))
        sum_ref[pl.ds(step, beams, stride=PITCH), :] = by_real + crossed
    for index in range(beams):
        out_ref[index, 0] = sum_ref[pl.ds(PITCH * index, near), :].astype(BF16)


def order_kernel(data_ref, out_ref):
    coarse, frames, fine = out_ref.shape[2:]
    width = 2 * frames
    row = lax.broadcasted_iota(jnp.int32, (width, LANES), 0)
    column = lax.broadcasted_iota(jnp.int32, (width, LANES), 1)
    unit = (row == column).astype(F32).astype(BF16)
    keep = lax.broadcasted_iota(jnp.int32, (fine, LANES), 1) < width
    for index in range(coarse):
        block = data_ref[:, 0, :, index].astype(F32).reshape(fine, LANES)
        block = jnp.where(keep, block, 0.0).astype(BF16)
        found = lax.dot_general(unit, block, NT, preferred_element_type=F32)
        out_ref[0, 0, index] = found[:frames]
        out_ref[0, 1, index] = found[frames:]


def in_hbm(array):
    return pltpu.with_memory_space_constraint(array, pltpu.HBM)


def body(volts, taps, delays, station_sub, beam_sub):
    count, fine = taps.shape
    stations, coarse, half = volts.shape[1:]
    beams = beam_sub.shape[0]
    stn, chan, beam = (lax.axis_size(name) for name in ("stn", "chan", "beam"))
    core = lax.axis_index("beam")
    dests = stn * beam
    near = fine // dests
    frames = beam * half // (3 * fine // 4)
    own = stations // beam
    amplitude = 1.0 / math.sqrt(stations * stn // SUBARRAYS)

    arranged = jnp.transpose(volts, (0, 2, 1, 3))
    away = lax.dynamic_slice_in_dim(arranged, (1 - core) * own, own, 2)
    other = lax.ppermute(away, "beam", [(0, 1), (1, 0)])

    code = jnp.where(station_sub[:, None] == beam_sub[None, :], delays.T, -1)
    code = code.reshape(stations // 4, 4, beams).transpose(1, 0, 2)
    copies = jnp.broadcast_to(code, (stn,) + code.shape)
    codes = lax.all_to_all(lax.optimization_barrier(copies), "stn", 0, 0, tiled=True)

    spectra = pl.pallas_call(
        channelize_kernel,
        grid=(coarse,),
        out_shape=pltpu.HBM((dests, coarse, own // 4 * near, 8 * frames), BF16),
        in_specs=[
            pl.BlockSpec(memory_space=pltpu.SMEM),
            pl.BlockSpec((2, 1, stations, half), lambda c: (0, c, 0, 0)),
            pl.BlockSpec((2, 1, own, half), lambda c: (0, c, 0, 0)),
            pl.BlockSpec((count, fine), lambda c: (0, 0)),
            pl.BlockSpec((fine, 2 * fine), lambda c: (0, 0)),
        ],
        out_specs=pl.BlockSpec((dests, 1, own // 4 * near, 8 * frames), lambda c: (0, c, 0, 0)),
        scratch_shapes=[
            pltpu.VMEM((2, own, beam * half), BF16),
            pltpu.VMEM((2 * fine // LANES, 4 * frames * PITCH, LANES), F32),
            pltpu.VMEM((4 * (count + 1), 8, fine), F32),
        ],
        compiler_params=pltpu.CompilerParams(vmem_limit_bytes=40 * 2**20),
        name="channelize",
    )(core.reshape(1), arranged, other, in_hbm(taps), in_hbm(dft_table(fine)))

    spectra, codes = lax.optimization_barrier((spectra, codes))
    mixed = lax.all_to_all(spectra, ("stn", "beam"), 0, 0, tiled=True)

    place = jnp.stack(
        [
            lax.axis_index("chan") * coarse,
            (lax.axis_index("stn") * beam + core) * near,
        ]
    ).astype(jnp.int32)
    total = stations * stn
    weights = pl.pallas_call(
        functools.partial(weight_kernel, amplitude, fine),
        grid=(coarse,),
        out_shape=pltpu.HBM((coarse, near, 2 * beams, total), BF16),
        in_specs=[
            pl.BlockSpec(memory_space=pltpu.SMEM),
            pl.BlockSpec((stn, 4, stations // 4, beams), lambda c: (0, 0, 0, 0)),
        ],
        out_specs=pl.BlockSpec((1, near, 2 * beams, total), lambda c: (c, 0, 0, 0)),
        scratch_shapes=[pltpu.VMEM((total, beams), jnp.int32)],
        compiler_params=pltpu.CompilerParams(vmem_limit_bytes=24 * 2**20),
        name="weights",
    )(place, codes)
    formed = pl.pallas_call(
        beam_kernel,
        grid=(coarse,),
        out_shape=jax.ShapeDtypeStruct((beams, coarse, near, LANES), BF16),
        in_specs=[
            pl.BlockSpec((1, near, 2 * beams, total), lambda c: (c, 0, 0, 0)),
            pl.BlockSpec((dests, 1, own // 4 * near, 8 * frames), lambda c: (0, c, 0, 0)),
        ],
        out_specs=pl.BlockSpec((beams, 1, near, LANES), lambda c: (0, c, 0, 0)),
        scratch_shapes=[
            pltpu.VMEM((3, total // 4 * PITCH, LANES), F32),
            pltpu.VMEM((beams * PITCH, LANES), F32),
        ],
        compiler_params=pltpu.CompilerParams(vmem_limit_bytes=24 * 2**20),
        name="beamform",
    )(in_hbm(weights), mixed)

    owned = lax.all_to_all(formed, ("stn", "chan", "beam"), 0, 0, tiled=True)
    owned = owned.reshape(stn, chan, beam, coarse, near, LANES)
    return pl.pallas_call(
        order_kernel,
        grid=(chan,),
        out_shape=jax.ShapeDtypeStruct((1, 2, chan * coarse, frames, fine), F32),
        in_specs=[
            pl.BlockSpec((stn, 1, beam, coarse, near, LANES), lambda z: (0, z, 0, 0, 0, 0))
        ],
        out_specs=pl.BlockSpec((1, 2, coarse, frames, fine), lambda z: (0, 0, z, 0, 0)),
        compiler_params=pltpu.CompilerParams(vmem_limit_bytes=32 * 2**20),
        name="order",
    )(owned)


def solution(mesh):
    placed = (P(None, "stn", "chan", "beam"), P(), P(None, "stn"), P("stn"), P())
    return jax.shard_map(
        body,
        mesh=mesh,
        in_specs=placed,
        out_specs=P(("stn", "chan", "beam"), None, None, None, None),
        check_vma=False,
    )
```

```python
import functools
import math

import jax
import jax.numpy as jnp
import ml_dtypes
import numpy as np
from jax import lax
from jax.experimental import pallas as pl
from jax.experimental.pallas import tpu as pltpu
from jax.sharding import PartitionSpec as P

SUBARRAYS = 4
F32 = jnp.float32
BF16 = jnp.bfloat16
LANES = 128
PITCH = 9
NT = (((1,), (1,)), ((), ()))
NN = (((1,), (0,)), ((), ()))
START = (0, 0, 1, 2)
OFFSET = (0, 192, 128, 64)


def fill_filter_tables(taps_ref, wide_ref):
    count, fine = taps_ref.shape
    taps = taps_ref[...]
    lane = lax.broadcasted_iota(jnp.int32, (1, fine), 1)
    for phase, offset in enumerate(OFFSET):
        rolled = pltpu.roll(taps, offset, 1) if offset else taps
        for tap in range(count + 1):
            early, late = rolled[min(tap, count - 1)], rolled[max(tap - 1, 0)]
            early = early[None] if tap < count else jnp.zeros((1, fine), F32)
            late = late[None] if tap > 0 else jnp.zeros((1, fine), F32)
            row = jnp.where(lane >= offset, early, late)
            wide_ref[phase * (count + 1) + tap] = jnp.broadcast_to(row, (8, fine))


def dft_table(fine):
    index = np.arange(fine)
    angle = 2.0 * np.pi * (index[:, None] * index[None, :] % fine) / fine
    table = np.concatenate([np.cos(angle), np.sin(angle)], axis=1) / math.sqrt(fine)
    return jnp.asarray(table.astype(np.float32).astype(ml_dtypes.bfloat16))


def tap_range(phase, tile, count):
    low, high = tile * LANES, (tile + 1) * LANES
    first = 1 if high <= OFFSET[phase] else 0
    last = count - 1 if low >= OFFSET[phase] else count
    return first, last


def channelize_kernel(
    core_ref,
    sub_ref,
    own_ref,
    other_ref,
    prototype_ref,
    dft_ref,
    delay_ref,
    out_ref,
    x_ref,
    z_ref,
    taps_ref,
):
    count = prototype_ref.shape[0]

    @pl.when(pl.program_id(0) == 0)
    def _():
        fill_filter_tables(prototype_ref, taps_ref)
        last = out_ref.shape[1] - 1
        code = steering_unit(core_ref[0] * 16, sub_ref, delay_ref)
        for dest in range(out_ref.shape[0]):
            out_ref[dest, last] = code

    half = own_ref.shape[-1]
    fine = taps_ref.shape[-1]
    blocks = 2 * half // fine
    groups = blocks // 3
    core = core_ref[0]
    own_at = pl.multiple_of(core * half, LANES)
    other_at = pl.multiple_of((1 - core) * half, LANES)
    own_row = pl.multiple_of(core * 16, 16)
    for part in range(2):
        x_ref[part, :, pl.ds(own_at, half)] = own_ref[part, 0, pl.ds(own_row, 16), :]
        x_ref[part, :, pl.ds(other_at, half)] = other_ref[part, 0]
    frames = 4 * groups
    rows = 2 * frames
    depth = PITCH * rows
    tiles = fine // LANES
    for tile in range(tiles):
        for group in range(groups):
            sums = [[[None, None] for _ in range(2)] for _ in range(4)]
            for step in range(count + 3):
                block = 3 * group + step
                if block >= blocks:
                    break
                uses = []
                for phase in range(4):
                    first, last = tap_range(phase, tile, count)
                    tap = step - START[phase]
                    if first <= tap <= last:
                        uses.append((phase, tap))
                if not uses:
                    continue
                at = block * fine + tile * LANES
                data = [x_ref[part, :, pl.ds(at, LANES)].astype(F32) for part in range(2)]
                for phase, tap in uses:
                    weight = taps_ref[phase * (count + 1) + tap, :, pl.ds(tile * LANES, LANES)]
                    for part in range(2):
                        for side in range(2):
                            term = weight * data[part][8 * side : 8 * side + 8]
                            old = sums[phase][part][side]
                            sums[phase][part][side] = term if old is None else old + term
            for phase in range(4):
                frame = 4 * group + phase
                for side in range(2):
                    real, imag = sums[phase][0][side], sums[phase][1][side]
                    base = side * depth + PITCH * frame
                    top = pl.ds(base, 8)
                    low = pl.ds(base + PITCH * frames, 8)
                    z_ref[tile, top, :] = real
                    z_ref[tiles + tile, top, :] = imag
                    z_ref[tile, low, :] = imag
                    z_ref[tiles + tile, low, :] = -real
    table = dft_ref[...]
    piece = rows // 3
    dests = out_ref.shape[0]
    for pair in range(2):
        results = []
        for quad in (2 * pair, 2 * pair + 1):
            order = []
            base = pair * depth + 4 * (quad % 2)
            for member in range(3):
                order.append((base + member, rows))
                order.append((base + 3 + PITCH * member * piece, piece))
            operand = jnp.concatenate(
                [
                    jnp.concatenate(
                        [z_ref[lane, pl.ds(start, size, stride=PITCH), :] for lane in range(2 * tiles)], axis=1
                    ).astype(BF16)
                    for start, size in order
                ],
                axis=0,
            )
            found = lax.dot_general(table, operand, NT, preferred_element_type=F32)
            results.append(found.reshape(dests, fine // dests, 4 * rows))
        for index, result in enumerate(results):
            unit = 4 * pl.program_id(0) + 2 * pair + index
            out_ref[:, unit] = result.astype(BF16)


def steering_unit(first, sub_ref, delay_ref):
    row = lax.broadcasted_iota(jnp.int32, (8, LANES), 0)
    left = lax.broadcasted_iota(jnp.int32, (8, LANES), 1) < LANES // 2
    tiles = []
    subs = jnp.zeros((8, LANES), jnp.int32)
    for side in range(2):
        pieces = []
        for member in (2 * side, 2 * side + 1):
            pieces.append(delay_ref[pl.ds(first + member, 4, stride=4), :])
            for quad in range(4):
                chosen = (row == (member % 2) * 4 + quad) & (left == (side == 0))
                subs = jnp.where(chosen, sub_ref[first + 4 * quad + member], subs)
        delay = jnp.concatenate(pieces, axis=0)
        tiles.append(lax.shift_left(128 + (delay & 127), lax.shift_right_logical(delay, 7)))
    return jnp.concatenate(tiles + [subs], axis=1).astype(F32).astype(BF16)


def delay_of(code):
    high = jnp.zeros_like(code)
    for power in range(8, 15):
        high = high + (code >= 2**power).astype(jnp.int32)
    return high * 128 + lax.shift_right_logical(code, high) - 128


def turn_parts(turn):
    quadrant = lax.shift_right_logical(turn + 8192, 14)
    x = (turn - quadrant * 16384).astype(F32) * (2.0 * math.pi / 65536.0)
    y = x * x
    sine = x * (1.0 + y * (-1.0 / 6 + y * (1.0 / 120 + y * (-1.0 / 5040 + y * (1.0 / 362880)))))
    cosine = 1.0 + y * (-0.5 + y * (1.0 / 24 + y * (-1.0 / 720 + y * (1.0 / 40320))))
    odd = (quadrant & 1) == 1
    cos_part = jnp.where(odd, sine, cosine)
    sin_part = jnp.where(odd, cosine, sine)
    cos_part = jnp.where(((quadrant + 1) & 2) == 2, -cos_part, cos_part)
    sin_part = jnp.where((quadrant & 2) == 2, -sin_part, sin_part)
    return cos_part, sin_part


def beam_kernel(
    amplitude,
    fine,
    place_ref,
    beam_sub_ref,
    code_ref,
    data_ref,
    out_ref,
    delay_ref,
    weight_ref,
    flat_ref,
    sum_ref,
):
    near, rows, stations = weight_ref.shape
    beams = rows // 2
    sources, quads = data_ref.shape[:2]
    depth = stations // 4
    coarse = pl.program_id(0)

    @pl.when(coarse == 0)
    def _():
        lane = lax.broadcasted_iota(jnp.int32, (8, LANES), 1)
        wanted = beam_sub_ref[...]
        for source in range(sources):
            subs = code_ref[source, 0, :, pl.ds(2 * LANES, LANES)].astype(F32)
            turned = pltpu.roll(subs, LANES // 2, 1)
            for side in range(2):
                value = code_ref[source, 0, :, pl.ds(side * LANES, LANES)].astype(F32)
                delay = delay_of(value.astype(jnp.int32))
                sub = jnp.where((lane < LANES // 2) == (side == 0), subs, turned)
                delay = jnp.where(sub == wanted, delay, -1)
                for index in range(2):
                    at = (2 * side + index) * depth + source * quads
                    delay_ref[pl.ds(at, quads), :] = delay[index * quads : (index + 1) * quads]

    freq = (place_ref[0] + coarse) * fine + place_ref[1]
    strip = 32
    for member in range(4):
        lanes = pl.ds(member * depth, depth)
        turned = jnp.transpose(delay_ref[lanes, :].astype(F32)).astype(jnp.int32)
        for top in range(0, beams, strip):
            delay = turned[top : top + strip]
            scale = jnp.where(delay >= 0, amplitude, 0.0).astype(F32)
            delay = jnp.maximum(delay, 0)
            cos_part, sin_part = turn_parts((delay * freq) & 65535)
            cos_step, sin_step = turn_parts(delay)
            real, imag = cos_part * scale, -(sin_part * scale)
            for step in range(near):
                weight_ref[step, pl.ds(top, strip), lanes] = real.astype(BF16)
                weight_ref[step, pl.ds(beams + top, strip), lanes] = imag.astype(BF16)
                if step + 1 < near:
                    real, imag = (
                        real * cos_step + imag * sin_step,
                        imag * cos_step - real * sin_step,
                    )

    for tile in range(3):
        for source in range(sources):
            for quad in range(quads):
                block = data_ref[source, quad, :, pl.ds(tile * LANES, LANES)].astype(F32)
                row = PITCH * (source * quads + quad)
                flat_ref[tile, pl.ds(row, near), :] = block
    lane = lax.broadcasted_iota(jnp.int32, (depth, LANES), 1)
    lane_out = lax.broadcasted_iota(jnp.int32, (beams, LANES), 1)
    for step in range(near):
        pieces = [flat_ref[tile, pl.ds(step, depth, stride=PITCH), :] for tile in range(3)]
        last = jnp.where(
            lane < 32,
            pltpu.roll(pieces[0], 32, 1),
            jnp.where(lane < 64, pltpu.roll(pieces[1], 64, 1), pltpu.roll(pieces[2], 96, 1)),
        )
        operand = jnp.concatenate([piece.astype(BF16) for piece in pieces + [last]], axis=0)
        found = lax.dot_general(weight_ref[step], operand, NN, preferred_element_type=F32)
        by_real, by_imag = found[:beams], found[beams:]
        crossed = jnp.where(lane_out < 48, -pltpu.roll(by_imag, 80, 1), pltpu.roll(by_imag, 48, 1))
        sum_ref[pl.ds(step, beams, stride=PITCH), :] = by_real + crossed
    for index in range(beams):
        out_ref[index, 0] = sum_ref[pl.ds(PITCH * index, near), :].astype(BF16)


def order_kernel(data_ref, out_ref):
    coarse, frames, fine = out_ref.shape[2:]
    width = 2 * frames
    row = lax.broadcasted_iota(jnp.int32, (width, LANES), 0)
    column = lax.broadcasted_iota(jnp.int32, (width, LANES), 1)
    unit = (row == column).astype(F32).astype(BF16)
    keep = lax.broadcasted_iota(jnp.int32, (fine, LANES), 1) < width
    for index in range(coarse):
        block = data_ref[:, 0, :, index].astype(F32).reshape(fine, LANES)
        block = jnp.where(keep, block, 0.0).astype(BF16)
        found = lax.dot_general(unit, block, NT, preferred_element_type=F32)
        out_ref[0, 0, index] = found[:frames]
        out_ref[0, 1, index] = found[frames:]


def in_hbm(array):
    return pltpu.with_memory_space_constraint(array, pltpu.HBM)


def body(volts, taps, delays, station_sub, beam_sub):
    count, fine = taps.shape
    stations, coarse, half = volts.shape[1:]
    beams = beam_sub.shape[0]
    stn, chan, beam = (lax.axis_size(name) for name in ("stn", "chan", "beam"))
    core = lax.axis_index("beam")
    dests = stn * beam
    near = fine // dests
    frames = beam * half // (3 * fine // 4)
    own = stations // beam
    amplitude = 1.0 / math.sqrt(stations * stn // SUBARRAYS)

    arranged = jnp.transpose(volts, (0, 2, 1, 3))
    away = lax.dynamic_slice_in_dim(arranged, (1 - core) * own, own, 2)
    other = lax.ppermute(away, "beam", [(0, 1), (1, 0)])

    quads = own // 4
    units = coarse * quads + 1

    spectra = pl.pallas_call(
        channelize_kernel,
        grid=(coarse,),
        out_shape=pltpu.HBM((dests, units, near, 8 * frames), BF16),
        in_specs=[
            pl.BlockSpec(memory_space=pltpu.SMEM),
            pl.BlockSpec(memory_space=pltpu.SMEM),
            pl.BlockSpec((2, 1, stations, half), lambda c: (0, c, 0, 0)),
            pl.BlockSpec((2, 1, own, half), lambda c: (0, c, 0, 0)),
            pl.BlockSpec((count, fine), lambda c: (0, 0)),
            pl.BlockSpec((fine, 2 * fine), lambda c: (0, 0)),
            pl.BlockSpec((stations, beams), lambda c: (0, 0)),
        ],
        out_specs=pl.BlockSpec((dests, units, near, 8 * frames), lambda c: (0, 0, 0, 0)),
        scratch_shapes=[
            pltpu.VMEM((2, own, beam * half), BF16),
            pltpu.VMEM((2 * fine // LANES, 4 * frames * PITCH, LANES), F32),
            pltpu.VMEM((4 * (count + 1), 8, fine), F32),
        ],
        compiler_params=pltpu.CompilerParams(vmem_limit_bytes=40 * 2**20),
        name="channelize",
    )(
        core.reshape(1),
        station_sub,
        arranged,
        other,
        in_hbm(taps),
        in_hbm(dft_table(fine)),
        in_hbm(delays.T),
    )

    mixed = lax.all_to_all(spectra, ("stn", "beam"), 0, 0, tiled=True)

    place = jnp.stack(
        [
            lax.axis_index("chan") * coarse,
            (lax.axis_index("stn") * beam + core) * near,
        ]
    ).astype(jnp.int32)
    total = stations * stn
    formed = pl.pallas_call(
        functools.partial(beam_kernel, amplitude, fine),
        grid=(coarse,),
        out_shape=jax.ShapeDtypeStruct((beams, coarse, near, LANES), BF16),
        in_specs=[
            pl.BlockSpec(memory_space=pltpu.SMEM),
            pl.BlockSpec((1, beams), lambda c: (0, 0)),
            pl.BlockSpec((dests, 1, near, 8 * frames), lambda c: (0, units - 1, 0, 0)),
            pl.BlockSpec((dests, quads, near, 8 * frames), lambda c: (0, c, 0, 0)),
        ],
        out_specs=pl.BlockSpec((beams, 1, near, LANES), lambda c: (0, c, 0, 0)),
        scratch_shapes=[
            pltpu.VMEM((total, beams), jnp.int32),
            pltpu.VMEM((near, 2 * beams, total), BF16),
            pltpu.VMEM((3, total // 4 * PITCH, LANES), F32),
            pltpu.VMEM((beams * PITCH, LANES), F32),
        ],
        compiler_params=pltpu.CompilerParams(vmem_limit_bytes=40 * 2**20),
        name="beamform",
    )(place, beam_sub.astype(F32).reshape(1, beams), mixed, mixed)

    owned = lax.all_to_all(formed, ("stn", "chan", "beam"), 0, 0, tiled=True)
    owned = owned.reshape(stn, chan, beam, coarse, near, LANES)
    return pl.pallas_call(
        order_kernel,
        grid=(chan,),
        out_shape=jax.ShapeDtypeStruct((1, 2, chan * coarse, frames, fine), F32),
        in_specs=[
            pl.BlockSpec((stn, 1, beam, coarse, near, LANES), lambda z: (0, z, 0, 0, 0, 0))
        ],
        out_specs=pl.BlockSpec((1, 2, coarse, frames, fine), lambda z: (0, 0, z, 0, 0)),
        compiler_params=pltpu.CompilerParams(vmem_limit_bytes=32 * 2**20),
        name="order",
    )(owned)


def solution(mesh):
    placed = (P(None, "stn", "chan", "beam"), P(), P(None, "stn"), P("stn"), P())
    return jax.shard_map(
        body,
        mesh=mesh,
        in_specs=placed,
        out_specs=P(("stn", "chan", "beam"), None, None, None, None),
        check_vma=False,
    )
```

```python
import functools
import math

import jax
import jax.numpy as jnp
import ml_dtypes
import numpy as np
from jax import lax
from jax.experimental import pallas as pl
from jax.experimental.pallas import tpu as pltpu
from jax.sharding import PartitionSpec as P

SUBARRAYS = 4
F32 = jnp.float32
BF16 = jnp.bfloat16
LANES = 128
PITCH = 9
NT = (((1,), (1,)), ((), ()))
NN = (((1,), (0,)), ((), ()))
START = (0, 0, 1, 2)
OFFSET = (0, 192, 128, 64)


def fill_filter_tables(taps_ref, wide_ref):
    count, fine = taps_ref.shape
    taps = taps_ref[...]
    lane = lax.broadcasted_iota(jnp.int32, (1, fine), 1)
    for phase, offset in enumerate(OFFSET):
        rolled = pltpu.roll(taps, offset, 1) if offset else taps
        for tap in range(count + 1):
            early, late = rolled[min(tap, count - 1)], rolled[max(tap - 1, 0)]
            early = early[None] if tap < count else jnp.zeros((1, fine), F32)
            late = late[None] if tap > 0 else jnp.zeros((1, fine), F32)
            row = jnp.where(lane >= offset, early, late)
            wide_ref[phase * (count + 1) + tap] = jnp.broadcast_to(row, (8, fine))


def dft_table(fine):
    index = np.arange(fine)
    angle = 2.0 * np.pi * (index[:, None] * index[None, :] % fine) / fine
    table = np.concatenate([np.cos(angle), np.sin(angle)], axis=1) / math.sqrt(fine)
    return jnp.asarray(table.astype(np.float32).astype(ml_dtypes.bfloat16))


def tap_range(phase, tile, count):
    low, high = tile * LANES, (tile + 1) * LANES
    first = 1 if high <= OFFSET[phase] else 0
    last = count - 1 if low >= OFFSET[phase] else count
    return first, last


def channelize_kernel(
    core_ref,
    sub_ref,
    own_ref,
    other_ref,
    prototype_ref,
    dft_ref,
    delay_ref,
    out_ref,
    x_ref,
    z_ref,
    taps_ref,
):
    count = prototype_ref.shape[0]

    @pl.when(pl.program_id(0) == 0)
    def _():
        fill_filter_tables(prototype_ref, taps_ref)
        last = out_ref.shape[1] - 1
        code = steering_unit(core_ref[0] * 16, sub_ref, delay_ref)
        for dest in range(out_ref.shape[0]):
            out_ref[dest, last] = code

    half = own_ref.shape[-1]
    fine = taps_ref.shape[-1]
    blocks = 2 * half // fine
    groups = blocks // 3
    core = core_ref[0]
    own_at = pl.multiple_of(core * half, LANES)
    other_at = pl.multiple_of((1 - core) * half, LANES)
    own_row = pl.multiple_of(core * 16, 16)
    for part in range(2):
        x_ref[part, :, pl.ds(own_at, half)] = own_ref[part, 0, pl.ds(own_row, 16), :]
        x_ref[part, :, pl.ds(other_at, half)] = other_ref[part, 0]
    frames = 4 * groups
    rows = 2 * frames
    depth = PITCH * rows
    tiles = fine // LANES
    for tile in range(tiles):
        for group in range(groups):
            sums = [[[None, None] for _ in range(2)] for _ in range(4)]
            for step in range(count + 3):
                block = 3 * group + step
                if block >= blocks:
                    break
                uses = []
                for phase in range(4):
                    first, last = tap_range(phase, tile, count)
                    tap = step - START[phase]
                    if first <= tap <= last:
                        uses.append((phase, tap))
                if not uses:
                    continue
                at = block * fine + tile * LANES
                data = [x_ref[part, :, pl.ds(at, LANES)].astype(F32) for part in range(2)]
                for phase, tap in uses:
                    weight = taps_ref[phase * (count + 1) + tap, :, pl.ds(tile * LANES, LANES)]
                    for part in range(2):
                        for side in range(2):
                            term = weight * data[part][8 * side : 8 * side + 8]
                            old = sums[phase][part][side]
                            sums[phase][part][side] = term if old is None else old + term
            for phase in range(4):
                frame = 4 * group + phase
                for side in range(2):
                    real, imag = sums[phase][0][side], sums[phase][1][side]
                    base = side * depth + PITCH * frame
                    top = pl.ds(base, 8)
                    low = pl.ds(base + PITCH * frames, 8)
                    z_ref[tile, top, :] = real
                    z_ref[tiles + tile, top, :] = imag
                    z_ref[tile, low, :] = imag
                    z_ref[tiles + tile, low, :] = -real
    table = dft_ref[...]
    piece = rows // 3
    dests = out_ref.shape[0]
    for pair in range(2):
        results = []
        for quad in (2 * pair, 2 * pair + 1):
            order = []
            base = pair * depth + 4 * (quad % 2)
            for member in range(3):
                order.append((base + member, rows))
                order.append((base + 3 + PITCH * member * piece, piece))
            operand = jnp.concatenate(
                [
                    jnp.concatenate(
                        [z_ref[lane, pl.ds(start, size, stride=PITCH), :] for lane in range(2 * tiles)], axis=1
                    ).astype(BF16)
                    for start, size in order
                ],
                axis=0,
            )
            found = lax.dot_general(table, operand, NT, preferred_element_type=F32)
            results.append(found.reshape(dests, fine // dests, 4 * rows))
        for index, result in enumerate(results):
            unit = 4 * pl.program_id(0) + 2 * pair + index
            out_ref[:, unit] = result.astype(BF16)


def steering_unit(first, sub_ref, delay_ref):
    row = lax.broadcasted_iota(jnp.int32, (8, LANES), 0)
    left = lax.broadcasted_iota(jnp.int32, (8, LANES), 1) < LANES // 2
    tiles = []
    subs = jnp.zeros((8, LANES), jnp.int32)
    for side in range(2):
        pieces = []
        for member in (2 * side, 2 * side + 1):
            pieces.append(delay_ref[pl.ds(first + member, 4, stride=4), :])
            for quad in range(4):
                chosen = (row == (member % 2) * 4 + quad) & (left == (side == 0))
                subs = jnp.where(chosen, sub_ref[first + 4 * quad + member], subs)
        delay = jnp.concatenate(pieces, axis=0)
        tiles.append(lax.shift_left(128 + (delay & 127), lax.shift_right_logical(delay, 7)))
    return jnp.concatenate(tiles + [subs], axis=1).astype(F32).astype(BF16)


def delay_of(code):
    high = jnp.zeros_like(code)
    for power in range(8, 15):
        high = high + (code >= 2**power).astype(jnp.int32)
    return high * 128 + lax.shift_right_logical(code, high) - 128


def turn_parts(turn):
    quadrant = lax.shift_right_logical(turn + 8192, 14)
    x = (turn - quadrant * 16384).astype(F32) * (2.0 * math.pi / 65536.0)
    y = x * x
    sine = x * (1.0 + y * (-1.0 / 6 + y * (1.0 / 120 + y * (-1.0 / 5040 + y * (1.0 / 362880)))))
    cosine = 1.0 + y * (-0.5 + y * (1.0 / 24 + y * (-1.0 / 720 + y * (1.0 / 40320))))
    odd = (quadrant & 1) == 1
    cos_part = jnp.where(odd, sine, cosine)
    sin_part = jnp.where(odd, cosine, sine)
    cos_part = jnp.where(((quadrant + 1) & 2) == 2, -cos_part, cos_part)
    sin_part = jnp.where((quadrant & 2) == 2, -sin_part, sin_part)
    return cos_part, sin_part


def beam_kernel(
    amplitude,
    fine,
    place_ref,
    beam_sub_ref,
    code_ref,
    data_ref,
    out_ref,
    delay_ref,
    state_ref,
    weight_ref,
    flat_ref,
    sum_ref,
):
    near, rows, stations = weight_ref.shape
    beams = rows // 2
    sources, quads = data_ref.shape[:2]
    depth = stations // 4
    coarse = pl.program_id(0)

    @pl.when(coarse == 0)
    def _():
        lane = lax.broadcasted_iota(jnp.int32, (8, LANES), 1)
        wanted = beam_sub_ref[...]
        for source in range(sources):
            subs = code_ref[source, 0, :, pl.ds(2 * LANES, LANES)].astype(F32)
            turned = pltpu.roll(subs, LANES // 2, 1)
            for side in range(2):
                value = code_ref[source, 0, :, pl.ds(side * LANES, LANES)].astype(F32)
                delay = delay_of(value.astype(jnp.int32))
                sub = jnp.where((lane < LANES // 2) == (side == 0), subs, turned)
                delay = jnp.where(sub == wanted, delay, -1)
                for index in range(2):
                    at = (2 * side + index) * depth + source * quads
                    delay_ref[pl.ds(at, quads), :] = delay[index * quads : (index + 1) * quads]

    strip = 16

    @pl.when(coarse == 0)
    def _():
        freq = place_ref[0] * fine + place_ref[1]
        for member in range(4):
            lanes = pl.ds(member * depth, depth)
            turned = jnp.transpose(delay_ref[lanes, :].astype(F32)).astype(jnp.int32)
            for top in range(0, beams, strip):
                delay = turned[top : top + strip]
                scale = jnp.where(delay >= 0, amplitude, 0.0).astype(F32)
                delay = jnp.maximum(delay, 0)
                cos_part, sin_part = turn_parts((delay * freq) & 65535)
                parts = (cos_part * scale, -(sin_part * scale))
                parts = parts + turn_parts(delay) + turn_parts((delay * fine) & 65535)
                for index, part in enumerate(parts):
                    state_ref[index, pl.ds(top, strip), lanes] = part

    for member in range(4):
        lanes = pl.ds(member * depth, depth)
        for top in range(0, beams, strip):
            here = (pl.ds(top, strip), lanes)
            first_real, first_imag, cos_step, sin_step, cos_jump, sin_jump = [
                state_ref[index, here[0], here[1]] for index in range(6)
            ]
            real, imag = first_real, first_imag
            for step in range(near):
                weight_ref[step, pl.ds(top, strip), lanes] = real.astype(BF16)
                weight_ref[step, pl.ds(beams + top, strip), lanes] = imag.astype(BF16)
                if step + 1 < near:
                    real, imag = (
                        real * cos_step + imag * sin_step,
                        imag * cos_step - real * sin_step,
                    )
            state_ref[0, here[0], here[1]] = first_real * cos_jump + first_imag * sin_jump
            state_ref[1, here[0], here[1]] = first_imag * cos_jump - first_real * sin_jump

    for tile in range(3):
        for source in range(sources):
            for quad in range(quads):
                block = data_ref[source, quad, :, pl.ds(tile * LANES, LANES)].astype(F32)
                row = PITCH * (source * quads + quad)
                flat_ref[tile, pl.ds(row, near), :] = block
    lane = lax.broadcasted_iota(jnp.int32, (depth, LANES), 1)
    lane_out = lax.broadcasted_iota(jnp.int32, (beams, LANES), 1)
    for step in range(near):
        pieces = [flat_ref[tile, pl.ds(step, depth, stride=PITCH), :] for tile in range(3)]
        last = jnp.where(
            lane < 32,
            pltpu.roll(pieces[0], 32, 1),
            jnp.where(lane < 64, pltpu.roll(pieces[1], 64, 1), pltpu.roll(pieces[2], 96, 1)),
        )
        operand = jnp.concatenate([piece.astype(BF16) for piece in pieces + [last]], axis=0)
        found = lax.dot_general(weight_ref[step], operand, NN, preferred_element_type=F32)
        by_real, by_imag = found[:beams], found[beams:]
        crossed = jnp.where(lane_out < 48, -pltpu.roll(by_imag, 80, 1), pltpu.roll(by_imag, 48, 1))
        sum_ref[pl.ds(step, beams, stride=PITCH), :] = by_real + crossed
    for index in range(beams):
        out_ref[index, 0] = sum_ref[pl.ds(PITCH * index, near), :].astype(BF16)


def order_kernel(data_ref, out_ref):
    coarse, frames, fine = out_ref.shape[2:]
    width = 2 * frames
    row = lax.broadcasted_iota(jnp.int32, (width, LANES), 0)
    column = lax.broadcasted_iota(jnp.int32, (width, LANES), 1)
    unit = (row == column).astype(F32).astype(BF16)
    keep = lax.broadcasted_iota(jnp.int32, (fine, LANES), 1) < width
    for index in range(coarse):
        block = data_ref[:, 0, :, index].astype(F32).reshape(fine, LANES)
        block = jnp.where(keep, block, 0.0).astype(BF16)
        found = lax.dot_general(unit, block, NT, preferred_element_type=F32)
        out_ref[0, 0, index] = found[:frames]
        out_ref[0, 1, index] = found[frames:]


def in_hbm(array):
    return pltpu.with_memory_space_constraint(array, pltpu.HBM)


def body(volts, taps, delays, station_sub, beam_sub):
    count, fine = taps.shape
    stations, coarse, half = volts.shape[1:]
    beams = beam_sub.shape[0]
    stn, chan, beam = (lax.axis_size(name) for name in ("stn", "chan", "beam"))
    core = lax.axis_index("beam")
    dests = stn * beam
    near = fine // dests
    frames = beam * half // (3 * fine // 4)
    own = stations // beam
    amplitude = 1.0 / math.sqrt(stations * stn // SUBARRAYS)

    arranged = jnp.transpose(volts, (0, 2, 1, 3))
    away = lax.dynamic_slice_in_dim(arranged, (1 - core) * own, own, 2)
    other = lax.ppermute(away, "beam", [(0, 1), (1, 0)])

    quads = own // 4
    units = coarse * quads + 1

    spectra = pl.pallas_call(
        channelize_kernel,
        grid=(coarse,),
        out_shape=pltpu.HBM((dests, units, near, 8 * frames), BF16),
        in_specs=[
            pl.BlockSpec(memory_space=pltpu.SMEM),
            pl.BlockSpec(memory_space=pltpu.SMEM),
            pl.BlockSpec((2, 1, stations, half), lambda c: (0, c, 0, 0)),
            pl.BlockSpec((2, 1, own, half), lambda c: (0, c, 0, 0)),
            pl.BlockSpec((count, fine), lambda c: (0, 0)),
            pl.BlockSpec((fine, 2 * fine), lambda c: (0, 0)),
            pl.BlockSpec((stations, beams), lambda c: (0, 0)),
        ],
        out_specs=pl.BlockSpec((dests, units, near, 8 * frames), lambda c: (0, 0, 0, 0)),
        scratch_shapes=[
            pltpu.VMEM((2, own, beam * half), BF16),
            pltpu.VMEM((2 * fine // LANES, 4 * frames * PITCH, LANES), F32),
            pltpu.VMEM((4 * (count + 1), 8, fine), F32),
        ],
        compiler_params=pltpu.CompilerParams(vmem_limit_bytes=40 * 2**20),
        name="channelize",
    )(
        core.reshape(1),
        station_sub,
        arranged,
        other,
        in_hbm(taps),
        in_hbm(dft_table(fine)),
        in_hbm(delays.T),
    )

    mixed = lax.all_to_all(spectra, ("stn", "beam"), 0, 0, tiled=True)

    place = jnp.stack(
        [
            lax.axis_index("chan") * coarse,
            (lax.axis_index("stn") * beam + core) * near,
        ]
    ).astype(jnp.int32)
    total = stations * stn
    formed = pl.pallas_call(
        functools.partial(beam_kernel, amplitude, fine),
        grid=(coarse,),
        out_shape=jax.ShapeDtypeStruct((beams, coarse, near, LANES), BF16),
        in_specs=[
            pl.BlockSpec(memory_space=pltpu.SMEM),
            pl.BlockSpec((1, beams), lambda c: (0, 0)),
            pl.BlockSpec((dests, 1, near, 8 * frames), lambda c: (0, units - 1, 0, 0)),
            pl.BlockSpec((dests, quads, near, 8 * frames), lambda c: (0, c, 0, 0)),
        ],
        out_specs=pl.BlockSpec((beams, 1, near, LANES), lambda c: (0, c, 0, 0)),
        scratch_shapes=[
            pltpu.VMEM((total, beams), jnp.int32),
            pltpu.VMEM((6, beams, total), F32),
            pltpu.VMEM((near, 2 * beams, total), BF16),
            pltpu.VMEM((3, total // 4 * PITCH, LANES), F32),
            pltpu.VMEM((beams * PITCH, LANES), F32),
        ],
        compiler_params=pltpu.CompilerParams(vmem_limit_bytes=40 * 2**20),
        name="beamform",
    )(place, beam_sub.astype(F32).reshape(1, beams), mixed, mixed)

    owned = lax.all_to_all(formed, ("stn", "chan", "beam"), 0, 0, tiled=True)
    owned = owned.reshape(stn, chan, beam, coarse, near, LANES)
    return pl.pallas_call(
        order_kernel,
        grid=(chan,),
        out_shape=jax.ShapeDtypeStruct((1, 2, chan * coarse, frames, fine), F32),
        in_specs=[
            pl.BlockSpec((stn, 1, beam, coarse, near, LANES), lambda z: (0, z, 0, 0, 0, 0))
        ],
        out_specs=pl.BlockSpec((1, 2, coarse, frames, fine), lambda z: (0, 0, z, 0, 0)),
        compiler_params=pltpu.CompilerParams(vmem_limit_bytes=32 * 2**20),
        name="order",
    )(owned)


def solution(mesh):
    placed = (P(None, "stn", "chan", "beam"), P(), P(None, "stn"), P("stn"), P())
    return jax.shard_map(
        body,
        mesh=mesh,
        in_specs=placed,
        out_specs=P(("stn", "chan", "beam"), None, None, None, None),
        check_vma=False,
    )
```

```python
import functools
import math

import jax
import jax.numpy as jnp
import ml_dtypes
import numpy as np
from jax import lax
from jax.experimental import pallas as pl
from jax.experimental.pallas import tpu as pltpu
from jax.sharding import PartitionSpec as P

SUBARRAYS = 4
F32 = jnp.float32
BF16 = jnp.bfloat16
LANES = 128
PITCH = 9
NT = (((1,), (1,)), ((), ()))
NN = (((1,), (0,)), ((), ()))
START = (0, 0, 1, 2)
OFFSET = (0, 192, 128, 64)


def fill_filter_tables(taps_ref, wide_ref):
    count, fine = taps_ref.shape
    taps = taps_ref[...]
    lane = lax.broadcasted_iota(jnp.int32, (1, fine), 1)
    for phase, offset in enumerate(OFFSET):
        rolled = pltpu.roll(taps, offset, 1) if offset else taps
        for tap in range(count + 1):
            early, late = rolled[min(tap, count - 1)], rolled[max(tap - 1, 0)]
            early = early[None] if tap < count else jnp.zeros((1, fine), F32)
            late = late[None] if tap > 0 else jnp.zeros((1, fine), F32)
            row = jnp.where(lane >= offset, early, late)
            wide_ref[phase * (count + 1) + tap] = jnp.broadcast_to(row, (8, fine))


def dft_table(fine):
    index = np.arange(fine)
    angle = 2.0 * np.pi * (index[:, None] * index[None, :] % fine) / fine
    table = np.concatenate([np.cos(angle), np.sin(angle)], axis=1) / math.sqrt(fine)
    return jnp.asarray(table.astype(np.float32).astype(ml_dtypes.bfloat16))


def tap_range(phase, tile, count):
    low, high = tile * LANES, (tile + 1) * LANES
    first = 1 if high <= OFFSET[phase] else 0
    last = count - 1 if low >= OFFSET[phase] else count
    return first, last


def channelize_kernel(
    core_ref,
    sub_ref,
    own_ref,
    other_ref,
    prototype_ref,
    dft_ref,
    delay_ref,
    out_ref,
    x_ref,
    z_ref,
    taps_ref,
):
    count = prototype_ref.shape[0]

    @pl.when(pl.program_id(0) == 0)
    def _():
        fill_filter_tables(prototype_ref, taps_ref)
        last = out_ref.shape[1] - 1
        code = steering_unit(core_ref[0] * 16, sub_ref, delay_ref)
        for dest in range(out_ref.shape[0]):
            out_ref[dest, last] = code

    half = own_ref.shape[-1]
    fine = taps_ref.shape[-1]
    blocks = 2 * half // fine
    groups = blocks // 3
    core = core_ref[0]
    own_at = pl.multiple_of(core * half, LANES)
    other_at = pl.multiple_of((1 - core) * half, LANES)
    own_row = pl.multiple_of(core * 16, 16)
    for part in range(2):
        x_ref[part, :, pl.ds(own_at, half)] = own_ref[part, 0, pl.ds(own_row, 16), :]
        x_ref[part, :, pl.ds(other_at, half)] = other_ref[part, 0]
    frames = 4 * groups
    rows = 2 * frames
    depth = PITCH * rows
    tiles = fine // LANES
    for tile in range(tiles):
        for group in range(groups):
            sums = [[[None, None] for _ in range(2)] for _ in range(4)]
            for step in range(count + 3):
                block = 3 * group + step
                if block >= blocks:
                    break
                uses = []
                for phase in range(4):
                    first, last = tap_range(phase, tile, count)
                    tap = step - START[phase]
                    if first <= tap <= last:
                        uses.append((phase, tap))
                if not uses:
                    continue
                at = block * fine + tile * LANES
                data = [x_ref[part, :, pl.ds(at, LANES)].astype(F32) for part in range(2)]
                for phase, tap in uses:
                    weight = taps_ref[phase * (count + 1) + tap, :, pl.ds(tile * LANES, LANES)]
                    for part in range(2):
                        for side in range(2):
                            term = weight * data[part][8 * side : 8 * side + 8]
                            old = sums[phase][part][side]
                            sums[phase][part][side] = term if old is None else old + term
            for phase in range(4):
                frame = 4 * group + phase
                for side in range(2):
                    real, imag = sums[phase][0][side], sums[phase][1][side]
                    base = side * depth + PITCH * frame
                    top = pl.ds(base, 8)
                    low = pl.ds(base + PITCH * frames, 8)
                    z_ref[tile, top, :] = real
                    z_ref[tiles + tile, top, :] = imag
                    z_ref[tile, low, :] = imag
                    z_ref[tiles + tile, low, :] = -real
    table = dft_ref[...]
    piece = rows // 3
    dests = out_ref.shape[0]
    for pair in range(2):
        results = []
        for quad in (2 * pair, 2 * pair + 1):
            order = []
            base = pair * depth + 4 * (quad % 2)
            for member in range(3):
                order.append((base + member, rows))
                order.append((base + 3 + PITCH * member * piece, piece))
            operand = jnp.concatenate(
                [
                    jnp.concatenate(
                        [z_ref[lane, pl.ds(start, size, stride=PITCH), :] for lane in range(2 * tiles)], axis=1
                    ).astype(BF16)
                    for start, size in order
                ],
                axis=0,
            )
            found = lax.dot_general(table, operand, NT, preferred_element_type=F32)
            results.append(found.reshape(dests, fine // dests, 4 * rows))
        for index, result in enumerate(results):
            unit = 4 * pl.program_id(0) + 2 * pair + index
            out_ref[:, unit] = result.astype(BF16)


def steering_unit(first, sub_ref, delay_ref):
    row = lax.broadcasted_iota(jnp.int32, (8, LANES), 0)
    left = lax.broadcasted_iota(jnp.int32, (8, LANES), 1) < LANES // 2
    tiles = []
    subs = jnp.zeros((8, LANES), jnp.int32)
    for side in range(2):
        pieces = []
        for member in (2 * side, 2 * side + 1):
            pieces.append(delay_ref[pl.ds(first + member, 4, stride=4), :])
            for quad in range(4):
                chosen = (row == (member % 2) * 4 + quad) & (left == (side == 0))
                subs = jnp.where(chosen, sub_ref[first + 4 * quad + member], subs)
        delay = jnp.concatenate(pieces, axis=0)
        tiles.append(lax.shift_left(128 + (delay & 127), lax.shift_right_logical(delay, 7)))
    return jnp.concatenate(tiles + [subs], axis=1).astype(F32).astype(BF16)


def delay_of(code):
    high = jnp.zeros_like(code)
    for power in range(8, 15):
        high = high + (code >= 2**power).astype(jnp.int32)
    return high * 128 + lax.shift_right_logical(code, high) - 128


def turn_parts(turn):
    quadrant = lax.shift_right_logical(turn + 8192, 14)
    x = (turn - quadrant * 16384).astype(F32) * (2.0 * math.pi / 65536.0)
    y = x * x
    sine = x * (1.0 + y * (-1.0 / 6 + y * (1.0 / 120 + y * (-1.0 / 5040 + y * (1.0 / 362880)))))
    cosine = 1.0 + y * (-0.5 + y * (1.0 / 24 + y * (-1.0 / 720 + y * (1.0 / 40320))))
    odd = (quadrant & 1) == 1
    cos_part = jnp.where(odd, sine, cosine)
    sin_part = jnp.where(odd, cosine, sine)
    cos_part = jnp.where(((quadrant + 1) & 2) == 2, -cos_part, cos_part)
    sin_part = jnp.where((quadrant & 2) == 2, -sin_part, sin_part)
    return cos_part, sin_part


def beam_kernel(
    amplitude,
    fine,
    place_ref,
    beam_sub_ref,
    code_ref,
    data_ref,
    out_ref,
    delay_ref,
    state_ref,
    weight_ref,
    flat_ref,
    sum_ref,
):
    near, rows, stations = weight_ref.shape
    beams = rows // 2
    sources, quads = data_ref.shape[:2]
    depth = stations // 4
    coarse = pl.program_id(0)

    @pl.when(coarse == 0)
    def _():
        lane = lax.broadcasted_iota(jnp.int32, (8, LANES), 1)
        wanted = beam_sub_ref[...]
        for source in range(sources):
            subs = code_ref[source, 0, :, pl.ds(2 * LANES, LANES)].astype(F32)
            turned = pltpu.roll(subs, LANES // 2, 1)
            for side in range(2):
                value = code_ref[source, 0, :, pl.ds(side * LANES, LANES)].astype(F32)
                delay = delay_of(value.astype(jnp.int32))
                sub = jnp.where((lane < LANES // 2) == (side == 0), subs, turned)
                delay = jnp.where(sub == wanted, delay, -1)
                for index in range(2):
                    at = (2 * side + index) * depth + source * quads
                    delay_ref[pl.ds(at, quads), :] = delay[index * quads : (index + 1) * quads]

    strip = 16

    @pl.when(coarse == 0)
    def _():
        freq = place_ref[0] * fine + place_ref[1]
        for member in range(4):
            lanes = pl.ds(member * depth, depth)
            turned = jnp.transpose(delay_ref[lanes, :].astype(F32)).astype(jnp.int32)
            for top in range(0, beams, strip):
                delay = turned[top : top + strip]
                scale = jnp.where(delay >= 0, amplitude, 0.0).astype(F32)
                delay = jnp.maximum(delay, 0)
                cos_part, sin_part = turn_parts((delay * freq) & 65535)
                parts = (cos_part * scale, -(sin_part * scale))
                parts = parts + turn_parts(delay) + turn_parts((delay * fine) & 65535)
                for index, part in enumerate(parts):
                    state_ref[index, pl.ds(top, strip), lanes] = part

    for member in range(4):
        lanes = pl.ds(member * depth, depth)
        for top in range(0, beams, strip):
            here = (pl.ds(top, strip), lanes)
            first_real, first_imag, cos_step, sin_step, cos_jump, sin_jump = [
                state_ref[index, here[0], here[1]] for index in range(6)
            ]
            real, imag = first_real, first_imag
            for step in range(near):
                weight_ref[step, pl.ds(top, strip), lanes] = real.astype(BF16)
                weight_ref[step, pl.ds(beams + top, strip), lanes] = imag.astype(BF16)
                if step + 1 < near:
                    real, imag = (
                        real * cos_step + imag * sin_step,
                        imag * cos_step - real * sin_step,
                    )
            state_ref[0, here[0], here[1]] = first_real * cos_jump + first_imag * sin_jump
            state_ref[1, here[0], here[1]] = first_imag * cos_jump - first_real * sin_jump

    for tile in range(3):
        for source in range(sources):
            for quad in range(quads):
                block = data_ref[source, quad, :, pl.ds(tile * LANES, LANES)].astype(F32)
                row = PITCH * (source * quads + quad)
                flat_ref[tile, pl.ds(row, near), :] = block
    lane = lax.broadcasted_iota(jnp.int32, (depth, LANES), 1)
    lane_out = lax.broadcasted_iota(jnp.int32, (beams, LANES), 1)
    for step in range(near):
        pieces = [flat_ref[tile, pl.ds(step, depth, stride=PITCH), :] for tile in range(3)]
        last = jnp.where(
            lane < 32,
            pltpu.roll(pieces[0], 32, 1),
            jnp.where(lane < 64, pltpu.roll(pieces[1], 64, 1), pltpu.roll(pieces[2], 96, 1)),
        )
        operand = jnp.concatenate([piece.astype(BF16) for piece in pieces + [last]], axis=0)
        found = lax.dot_general(weight_ref[step], operand, NN, preferred_element_type=F32)
        by_real, by_imag = found[:beams], found[beams:]
        crossed = jnp.where(lane_out < 48, -pltpu.roll(by_imag, 80, 1), pltpu.roll(by_imag, 48, 1))
        sum_ref[pl.ds(step, beams, stride=PITCH), :] = by_real + crossed
    for index in range(beams):
        out_ref[index, 0] = sum_ref[pl.ds(PITCH * index, near), :].astype(BF16)


def order_kernel(data_ref, out_ref):
    coarse, frames, fine = out_ref.shape[2:]
    width = 2 * frames
    row = lax.broadcasted_iota(jnp.int32, (width, LANES), 0)
    column = lax.broadcasted_iota(jnp.int32, (width, LANES), 1)
    unit = (row == column).astype(F32).astype(BF16)
    keep = lax.broadcasted_iota(jnp.int32, (fine, LANES), 1) < width
    for index in range(coarse):
        block = data_ref[:, 0, :, index].astype(F32).reshape(fine, LANES)
        block = jnp.where(keep, block, 0.0).astype(BF16)
        found = lax.dot_general(unit, block, NT, preferred_element_type=F32)
        out_ref[0, 0, index] = found[:frames]
        out_ref[0, 1, index] = found[frames:]


def in_hbm(array):
    return pltpu.with_memory_space_constraint(array, pltpu.HBM)


def body(volts, taps, delays, station_sub, beam_sub):
    count, fine = taps.shape
    stations, coarse, half = volts.shape[1:]
    beams = beam_sub.shape[0]
    stn, chan, beam = (lax.axis_size(name) for name in ("stn", "chan", "beam"))
    core = lax.axis_index("beam")
    dests = stn * beam
    near = fine // dests
    frames = beam * half // (3 * fine // 4)
    own = stations // beam
    amplitude = 1.0 / math.sqrt(stations * stn // SUBARRAYS)

    arranged = jnp.transpose(volts, (0, 2, 1, 3))
    away = lax.dynamic_slice_in_dim(arranged, (1 - core) * own, own, 2)
    other = lax.ppermute(away, "beam", [(0, 1), (1, 0)])

    quads = own // 4
    units = coarse * quads + 1

    spectra = pl.pallas_call(
        channelize_kernel,
        grid=(coarse,),
        out_shape=jax.ShapeDtypeStruct((dests, units, near, 8 * frames), BF16),
        in_specs=[
            pl.BlockSpec(memory_space=pltpu.SMEM),
            pl.BlockSpec(memory_space=pltpu.SMEM),
            pl.BlockSpec((2, 1, stations, half), lambda c: (0, c, 0, 0)),
            pl.BlockSpec((2, 1, own, half), lambda c: (0, c, 0, 0)),
            pl.BlockSpec((count, fine), lambda c: (0, 0)),
            pl.BlockSpec((fine, 2 * fine), lambda c: (0, 0)),
            pl.BlockSpec((stations, beams), lambda c: (0, 0)),
        ],
        out_specs=pl.BlockSpec((dests, units, near, 8 * frames), lambda c: (0, 0, 0, 0)),
        scratch_shapes=[
            pltpu.VMEM((2, own, beam * half), BF16),
            pltpu.VMEM((2 * fine // LANES, 4 * frames * PITCH, LANES), F32),
            pltpu.VMEM((4 * (count + 1), 8, fine), F32),
        ],
        compiler_params=pltpu.CompilerParams(vmem_limit_bytes=40 * 2**20),
        name="channelize",
    )(
        core.reshape(1),
        station_sub,
        arranged,
        other,
        in_hbm(taps),
        in_hbm(dft_table(fine)),
        in_hbm(delays.T),
    )

    place = jnp.stack(
        [
            lax.axis_index("chan") * coarse,
            (lax.axis_index("stn") * beam + core) * near,
        ]
    ).astype(jnp.int32)
    wanted = beam_sub.astype(F32).reshape(1, beams)
    spectra, place, wanted = lax.optimization_barrier((spectra, place, wanted))
    mixed = lax.all_to_all(spectra, ("stn", "beam"), 0, 0, tiled=True)

    total = stations * stn
    formed = pl.pallas_call(
        functools.partial(beam_kernel, amplitude, fine),
        grid=(coarse,),
        out_shape=jax.ShapeDtypeStruct((beams, coarse, near, LANES), BF16),
        in_specs=[
            pl.BlockSpec(memory_space=pltpu.SMEM),
            pl.BlockSpec((1, beams), lambda c: (0, 0)),
            pl.BlockSpec((dests, 1, near, 8 * frames), lambda c: (0, units - 1, 0, 0)),
            pl.BlockSpec((dests, quads, near, 8 * frames), lambda c: (0, c, 0, 0)),
        ],
        out_specs=pl.BlockSpec((beams, 1, near, LANES), lambda c: (0, c, 0, 0)),
        scratch_shapes=[
            pltpu.VMEM((total, beams), jnp.int32),
            pltpu.VMEM((6, beams, total), F32),
            pltpu.VMEM((near, 2 * beams, total), BF16),
            pltpu.VMEM((3, total // 4 * PITCH, LANES), F32),
            pltpu.VMEM((beams * PITCH, LANES), F32),
        ],
        compiler_params=pltpu.CompilerParams(vmem_limit_bytes=40 * 2**20),
        name="beamform",
    )(place, wanted, mixed, mixed)

    owned = lax.all_to_all(formed, ("stn", "chan", "beam"), 0, 0, tiled=True)
    owned = owned.reshape(stn, chan, beam, coarse, near, LANES)
    return pl.pallas_call(
        order_kernel,
        grid=(chan,),
        out_shape=jax.ShapeDtypeStruct((1, 2, chan * coarse, frames, fine), F32),
        in_specs=[
            pl.BlockSpec((stn, 1, beam, coarse, near, LANES), lambda z: (0, z, 0, 0, 0, 0))
        ],
        out_specs=pl.BlockSpec((1, 2, coarse, frames, fine), lambda z: (0, 0, z, 0, 0)),
        compiler_params=pltpu.CompilerParams(vmem_limit_bytes=32 * 2**20),
        name="order",
    )(owned)


def solution(mesh):
    placed = (P(None, "stn", "chan", "beam"), P(), P(None, "stn"), P("stn"), P())
    return jax.shard_map(
        body,
        mesh=mesh,
        in_specs=placed,
        out_specs=P(("stn", "chan", "beam"), None, None, None, None),
        check_vma=False,
    )
```
